32 devices in a mesh: grp: 2 (over x), aux: 8 (over z, y), bas: 2 (over core).
Axes of the slice: x: 2, y: 2, z: 4, core: 2. Of those that a mesh axis runs over, the one named last changes fastest.
Arguments:
- integrals: float32 [32, 16, 128, 1024], P(('grp', 'aux'), 'bas'), parts along dimension 0, may hold values from -0.1875 to 0.1875
- block_counts: int32 [32, 16], P(('grp', 'aux'), 'bas'), parts along dimension 0, may hold values from 1 to 8
- partner_blocks: int32 [32, 16, 8], P(('grp', 'aux'), 'bas'), parts along dimension 0, may hold values from 0 to 79, as said below
- occupied_coeff: float32 [20480, 512], P(('grp', 'bas')), parts along dimension 0, may hold values from -0.72 to 0.72
Outputs:
- exchange_matrix: float32 [4096, 2048], P(('grp', 'aux'), 'bas'), parts along dimension 0
The draws below stay inside these ranges and needn't reach their ends.
There are 2 independent parts, one for each index of `grp`. The reference program is written for one: setup_inputs(seed, part) draws one part's arguments, and reference() takes and returns one part's arrays. A program takes and returns all parts, laid end to end along the dimension named above; each array names one. Nothing has to cross between parts.
Inputs may be any that keep to these rules, and one draw needn't show every extreme that they name: `partner_blocks`: the 8 entries of a task's list are distinct shell block numbers; only the first block_counts of them are significant.
All inputs are finite; a program needn't handle non-finite values.
Results may differ from the reference program's by a relative error of at most 0.0003.
Values sent between devices are 32-bit elements; how exact they have to be, the bound alone decides.
A program may use at most 128 MiB of HBM per device.

```python
import jax
import jax.numpy as jnp
from jax import lax

SB = 128
NSB = 80
NOCC = 512
LMAX = 8
AUXD = 2
NAUXF = 16
WS = 16
NB = 10240


def draw_block_counts(key, part):
    key = jax.random.fold_in(key, 11)
    first_key, second_key, third_key = jax.random.split(key, 3)
    device_total = NAUXF // AUXD
    heavy_flags = jax.random.randint(first_key, (device_total,), 0, 4) == 0
    chosen_device = jax.random.randint(second_key, (), 0, device_total)
    heavy_flags = heavy_flags | (jnp.arange(device_total) == chosen_device)
    heavy_rows = jnp.repeat(heavy_flags, AUXD)
    light_counts = jax.random.randint(third_key, (NAUXF, WS), 1, LMAX // 2 + 1)
    return jnp.where(heavy_rows[:, None], LMAX, light_counts).astype(jnp.int32)


def draw_partner_blocks(key, part):
    key = jax.random.fold_in(key, 23)
    scores = jax.random.randint(key, (NAUXF, WS, NSB), 0, 2 ** 20) * NSB + jnp.arange(NSB)[None, None, :]
    top_scores, chosen_blocks = lax.top_k(scores, LMAX)
    return chosen_blocks.astype(jnp.int32)


def shard_levels(stream_key, dims, shards, smallest, top_value):
    def one(axis_at, blocks):
        steps = jax.random.uniform(jax.random.fold_in(jax.random.fold_in(stream_key, 6), axis_at), (blocks,), jnp.float32, smallest / len(shards), top_value / len(shards))
        return jnp.repeat(jnp.exp(steps), dims[axis_at] // blocks).reshape((-1,) + (1,) * (len(dims) - axis_at - 1))

    gain = one(*shards[0])
    for cut in shards[1:]:
        gain = gain * one(*cut)
    return gain


def normal_values(rng, extent, scale, limit, shards=(), dtype=jnp.bfloat16):
    drawn = scale * jax.random.normal(rng, extent, jnp.float32)
    if shards:
        drawn = drawn * shard_levels(rng, extent, shards, -0.22, 0.18)
    return jnp.clip(drawn, -limit, limit).astype(dtype)


def setup_inputs(seed: int = 0, part: int = 0) -> dict:
    keys = jax.random.split(jax.random.key(seed), 5)
    part_splits = jax.random.split(jax.random.fold_in(keys[4], part), 5)
    return {
        "integrals": normal_values(part_splits[0], (NAUXF, WS, SB, LMAX * SB), (LMAX * SB) ** -0.5, 0.1875, ((0, 8), (1, 2)), jnp.float32),
        "block_counts": draw_block_counts(jax.random.fold_in(jax.random.fold_in(keys[4], part), 71), part),
        "partner_blocks": draw_partner_blocks(jax.random.fold_in(jax.random.fold_in(keys[4], part), 71), part),
        "occupied_coeff": normal_values(part_splits[3], (NB, NOCC), 0.12, 0.72, ((0, 2),), jnp.float32),
    }


def half_rows(integral_block, count_row, list_row, coeff_blocks):
    mask_row = (jnp.arange(LMAX)[None, :] < count_row[:, None]).astype(jnp.float32)
    shaped = integral_block.reshape(WS, SB, LMAX, SB) * mask_row[:, None, :, None]
    picked = coeff_blocks[list_row]
    result = jnp.einsum("wmcl,wclo->wmo", shaped, picked, precision=lax.Precision.HIGHEST)
    return result.reshape(WS * SB, NOCC)


def reference(integrals, block_counts, partner_blocks, occupied_coeff):
    coeff_blocks = occupied_coeff.reshape(NSB, SB, NOCC)

    def accumulate(running, inputs):
        integral_block, count_row, list_row = inputs
        half_transformed = half_rows(integral_block, count_row, list_row, coeff_blocks)
        product = jnp.dot(half_transformed, half_transformed.T, precision=lax.Precision.HIGHEST, preferred_element_type=jnp.float32)
        return running + product, None

    initial = jnp.zeros((WS * SB, WS * SB), jnp.float32)
    exchange_matrix, unused = lax.scan(accumulate, initial, (integrals, block_counts, partner_blocks))
    return exchange_matrix
```

```python
import functools

import jax
import jax.numpy as jnp
from jax import lax
from jax.experimental import pallas as pl
from jax.experimental.pallas import tpu as pltpu
from jax.sharding import PartitionSpec as P

MESH = pl.DeviceIdType.MESH
VMEM_LIMIT = 58 * 1024 * 1024
PIECES = 4


def split(values):
    high = values.astype(jnp.bfloat16)
    low = (values - high.astype(jnp.float32)).astype(jnp.bfloat16)
    return high, low


def swap_kernel(pieces, mine_ref, other_ref, send_sem, recv_sem):
    partner = 1 - lax.axis_index("bas")
    barrier = pltpu.get_barrier_semaphore()
    pl.semaphore_signal(barrier, inc=1, device_id={"bas": partner}, device_id_type=MESH)
    pl.semaphore_wait(barrier, 1)
    rows = mine_ref.shape[0] // pieces
    copies = []
    for piece in range(pieces):
        part = pl.ds(piece * rows, rows)
        copy = pltpu.make_async_remote_copy(
            src_ref=mine_ref.at[part],
            dst_ref=other_ref.at[part],
            send_sem=send_sem.at[piece],
            recv_sem=recv_sem.at[piece],
            device_id={"bas": partner},
            device_id_type=MESH,
        )
        copy.start()
        copies.append(copy)
    for copy in copies:
        copy.wait()


def swap(mine):
    return pl.pallas_call(
        functools.partial(swap_kernel, PIECES),
        out_shape=jax.ShapeDtypeStruct(mine.shape, mine.dtype),
        in_specs=[pl.BlockSpec(memory_space=pl.ANY)],
        out_specs=pl.BlockSpec(memory_space=pl.ANY),
        scratch_shapes=[
            pltpu.SemaphoreType.DMA((PIECES,)),
            pltpu.SemaphoreType.DMA((PIECES,)),
        ],
        compiler_params=pltpu.CompilerParams(collective_id=0, has_side_effects=True),
        name="swap_coeff",
    )(mine)


def half_kernel(
    lists_ref, counts_ref, core_ref, tile_ref, mine_ref, other_ref, half_ref, rows_ref, sem
):
    task = pl.program_id(0)
    tasks = pl.num_programs(0)
    listed = lists_ref.shape[1]
    width = tile_ref.shape[0]
    local_blocks = mine_ref.shape[0] // width

    def fetch(which):
        slot = lax.rem(which, 2)
        for index in range(listed):
            block = lists_ref[which, index]
            owner = (block >= local_blocks).astype(jnp.int32)
            first = pl.multiple_of((block - owner * local_blocks) * width, width)
            place = rows_ref.at[slot, pl.ds(index * width, width)]

            @pl.when(owner == core_ref[0])
            def _():
                pltpu.make_async_copy(
                    mine_ref.at[pl.ds(first, width)], place, sem.at[slot]
                ).start()

            @pl.when(owner != core_ref[0])
            def _():
                pltpu.make_async_copy(
                    other_ref.at[pl.ds(first, width)], place, sem.at[slot]
                ).start()

    @pl.when(task == 0)
    def _():
        fetch(task)

    @pl.when(task + 1 < tasks)
    def _():
        fetch(task + 1)

    slot = lax.rem(task, 2)
    pltpu.make_async_copy(rows_ref.at[slot], rows_ref.at[slot], sem.at[slot]).wait()
    column = lax.broadcasted_iota(jnp.int32, tile_ref.shape, 1)
    tile = jnp.where(column < counts_ref[task] * width, tile_ref[...], 0.0)
    tile_high, tile_low = split(tile)
    row_high, row_low = split(rows_ref[slot])
    both = jnp.dot(
        jnp.concatenate([tile_high, tile_low], axis=0),
        row_high,
        preferred_element_type=jnp.float32,
    )
    cross = jnp.dot(tile_high, row_low, preferred_element_type=jnp.float32)
    half_ref[...] = both[:width] + (both[width:] + cross)


def half_all(tiles, counts, lists, mine, other):
    aux_local, shell_local, width, span = tiles.shape
    tasks = aux_local * shell_local
    occupied = mine.shape[1]
    core = lax.axis_index("bas").astype(jnp.int32).reshape(1)
    return pl.pallas_call(
        half_kernel,
        out_shape=jax.ShapeDtypeStruct((shell_local * width, aux_local * occupied), jnp.float32),
        grid_spec=pltpu.PrefetchScalarGridSpec(
            num_scalar_prefetch=3,
            grid=(tasks,),
            in_specs=[
                pl.BlockSpec((width, span), lambda task, *_: (task, 0)),
                pl.BlockSpec(memory_space=pl.ANY),
                pl.BlockSpec(memory_space=pl.ANY),
            ],
            out_specs=pl.BlockSpec(
                (width, occupied), lambda task, *_: (task % shell_local, task // shell_local)
            ),
            scratch_shapes=[
                pltpu.VMEM((2, span, occupied), jnp.float32),
                pltpu.SemaphoreType.DMA((2,)),
            ],
        ),
        compiler_params=pltpu.CompilerParams(vmem_limit_bytes=VMEM_LIMIT),
        name="half_transform",
    )(
        lists.reshape(tasks, lists.shape[2]),
        counts.reshape(tasks),
        core,
        tiles.reshape(tasks * width, span),
        mine,
        other,
    )


def exchange_kernel(
    aux,
    mine_ref,
    out_ref,
    other_ref,
    parts_ref,
    near_send,
    near_recv,
    sums_ref,
    far_recv,
    turn_send,
    turn_recv,
    half_sems,
    near_sems,
    far_sems,
    turn_sems,
):
    near_count = 2
    far_count = aux // near_count
    ring = aux // 2
    keep = ring // 2
    block = out_ref.shape[0]
    half_rows = mine_ref.shape[0]

    position = lax.axis_index("aux")
    core = lax.axis_index("bas")
    far = position // near_count
    near = lax.rem(position, near_count)

    barrier = pltpu.get_barrier_semaphore()
    me = position * 2 + core
    for step in range(1, 2 * aux):
        there = lax.rem(me + step, 2 * aux)
        pl.semaphore_signal(
            barrier,
            inc=1,
            device_id={"aux": there // 2, "bas": lax.rem(there, 2)},
            device_id_type=MESH,
        )
    pl.semaphore_wait(barrier, 2 * aux - 1)

    def remote(source, target, sems, index, device):
        return pltpu.make_async_remote_copy(
            src_ref=source,
            dst_ref=target,
            send_sem=sems.at[(0,) + index],
            recv_sem=sems.at[(1,) + index],
            device_id=device,
            device_id_type=MESH,
        )

    def half_copy(index):
        part = pl.ds(index * block, block)
        return remote(
            mine_ref.at[part], other_ref.at[part], half_sems, (index,), {"bas": 1 - core}
        )

    def near_copy(step, k):
        return remote(
            near_send.at[step, k],
            near_recv.at[step, k],
            near_sems,
            (step, k),
            {"aux": far * near_count + (1 - near)},
        )

    def far_copy(step, k):
        target = lax.rem(far + step + 1, far_count)
        return remote(
            sums_ref.at[step, k],
            far_recv.at[step, k],
            far_sems,
            (step, k),
            {"aux": target * near_count + near},
        )

    def in_half(far_index):
        return far_index // (far_count // 2) == core

    def column_of(row, k):
        local = lax.rem(row, ring)
        inside = (row // ring == core).astype(jnp.int32)
        return lax.rem(
            inside * (local + k) + (1 - inside) * (local - k - core + 2 * ring), ring
        )

    def turn_copy(k):
        inside = in_half(far).astype(jnp.int32)
        return remote(
            turn_send.at[k],
            turn_recv.at[k],
            turn_sems,
            (k,),
            {
                "aux": core * ring + column_of(position, k),
                "bas": inside * core + (1 - inside) * (1 - core),
            },
        )

    def blocks(far_index, work):
        for k in range(keep):
            work(k)
        pl.when(in_half(far_index))(functools.partial(work, keep))

    def store_parts(source, first, index):
        part = pl.ds(pl.multiple_of(index * block, block), block)
        high, low = split(source[part, :])
        start = pl.multiple_of((first + index) * 2 * block, 2 * block)
        parts_ref[pl.ds(start, block), :] = high
        parts_ref[pl.ds(start + block, block), :] = low

    def product(row, k):
        column = core * ring + column_of(row, k)
        row_at = pl.multiple_of(row * 2 * block, 2 * block)
        column_at = pl.multiple_of(column * 2 * block, 2 * block)
        contract = (((1,), (1,)), ((), ()))
        both = lax.dot_general(
            parts_ref[pl.ds(row_at, 2 * block), :],
            parts_ref[pl.ds(column_at, block), :],
            contract,
            preferred_element_type=jnp.float32,
        )
        cross = lax.dot_general(
            parts_ref[pl.ds(row_at, block), :],
            parts_ref[pl.ds(column_at + block, block), :],
            contract,
            preferred_element_type=jnp.float32,
        )
        return both[:block] + (both[block:] + cross)

    half_blocks = half_rows // block
    for index in range(half_blocks):
        half_copy(index).start()

    def split_mine(index, carry):
        store_parts(mine_ref, core * ring, index)
        return carry

    lax.fori_loop(0, half_blocks, split_mine, 0)

    def split_other(index, carry):
        half_copy(index).wait_recv()
        store_parts(other_ref, (1 - core) * ring, index)
        return carry

    lax.fori_loop(0, half_blocks, split_other, 0)

    def send_near(step, carry):
        target = lax.rem(far + step + 1, far_count)
        row = target * near_count + (1 - near)

        def work(k):
            near_send[step, k] = product(row, k)
            near_copy(step, k).start()

        blocks(target, work)
        return carry

    lax.fori_loop(0, far_count, send_near, 0)

    def own_products(step, carry):
        target = lax.rem(far + step + 1, far_count)

        def work(k):
            sums_ref[step, k] = product(target * near_count + near, k)

        blocks(target, work)
        return carry

    lax.fori_loop(0, far_count, own_products, 0)

    def send_far(step, carry):
        def work(k):
            near_copy(step, k).wait_recv()
            sums_ref[step, k] += near_recv[step, k]
            far_copy(step, k).start()

        blocks(lax.rem(far + step + 1, far_count), work)
        return carry

    lax.fori_loop(0, far_count - 1, send_far, 0)

    def finish(k):
        last = far_count - 1
        near_copy(last, k).wait_recv()
        total = sums_ref[last, k] + near_recv[last, k]
        for step in range(far_count - 1):
            far_copy(step, k).wait_recv()
            total += far_recv[step, k]
        at = pl.multiple_of(column_of(position, k) * block, block)
        out_ref[:, pl.ds(at, block)] = total
        return total

    def turned(k):
        turn_send[k] = finish(k).T
        turn_copy(k).start()

    def place(k):
        turn_copy(k).wait_recv()
        local = lax.rem(position, ring)
        inside = in_half(far).astype(jnp.int32)
        column = lax.rem(
            inside * (local - k + ring) + (1 - inside) * (local + k + 1 - core), ring
        )
        out_ref[:, pl.ds(pl.multiple_of(column * block, block), block)] = turn_recv[k]
        turn_copy(k).wait_send()

    here = in_half(far)
    there = jnp.logical_not(here)
    for k in range(1, keep):
        turned(k)

    @pl.when(here)
    def _():
        finish(0)
        finish(keep)

    pl.when(there)(functools.partial(turned, 0))
    for k in range(1, keep):
        place(k)
    pl.when(there)(functools.partial(place, 0))

    for index in range(half_blocks):
        half_copy(index).wait_send()

    def near_done(step, carry):
        blocks(
            lax.rem(far + step + 1, far_count), lambda k: near_copy(step, k).wait_send()
        )
        return carry

    lax.fori_loop(0, far_count, near_done, 0)

    def far_done(step, carry):
        blocks(
            lax.rem(far + step + 1, far_count), lambda k: far_copy(step, k).wait_send()
        )
        return carry

    lax.fori_loop(0, far_count - 1, far_done, 0)


def exchange(half, aux):
    half_rows, depth = half.shape
    block = 2 * half_rows // aux
    far_count = aux // 2
    slots = aux // 4 + 1
    square = (block, block)
    return pl.pallas_call(
        functools.partial(exchange_kernel, aux),
        out_shape=jax.ShapeDtypeStruct((block, half_rows), jnp.float32),
        in_specs=[pl.BlockSpec(memory_space=pltpu.VMEM)],
        out_specs=pl.BlockSpec(memory_space=pltpu.VMEM),
        scratch_shapes=[
            pltpu.VMEM((half_rows, depth), jnp.float32),
            pltpu.VMEM((4 * half_rows, depth), jnp.bfloat16),
            pltpu.VMEM((far_count, slots) + square, jnp.float32),
            pltpu.VMEM((far_count, slots) + square, jnp.float32),
            pltpu.VMEM((far_count, slots) + square, jnp.float32),
            pltpu.VMEM((far_count - 1, slots) + square, jnp.float32),
            pltpu.VMEM((slots,) + square, jnp.float32),
            pltpu.VMEM((slots,) + square, jnp.float32),
            pltpu.SemaphoreType.DMA((2, half_rows // block)),
            pltpu.SemaphoreType.DMA((2, far_count, slots)),
            pltpu.SemaphoreType.DMA((2, far_count - 1, slots)),
            pltpu.SemaphoreType.DMA((2, slots)),
        ],
        compiler_params=pltpu.CompilerParams(
            collective_id=1, has_side_effects=True, vmem_limit_bytes=VMEM_LIMIT
        ),
        name="exchange",
    )(half)


def shards(aux, integrals, block_counts, partner_blocks, occupied_coeff):
    other = swap(occupied_coeff)
    half = half_all(integrals, block_counts, partner_blocks, occupied_coeff, other)
    return exchange(half, aux)


def solution(mesh):
    placed = (
        P(("grp", "aux"), "bas", None, None),
        P(("grp", "aux"), "bas"),
        P(("grp", "aux"), "bas", None),
        P(("grp", "bas"), None),
    )
    return jax.shard_map(
        functools.partial(shards, mesh.shape["aux"]),
        mesh=mesh,
        in_specs=placed,
        out_specs=P(("grp", "aux"), "bas"),
        check_vma=False,
    )
```

```python
import functools

import jax
import jax.numpy as jnp
from jax import lax
from jax.experimental import pallas as pl
from jax.experimental.pallas import tpu as pltpu
from jax.sharding import PartitionSpec as P

MESH = pl.DeviceIdType.MESH
VMEM_LIMIT = 58 * 1024 * 1024
PIECES = 4


def split(values):
    high = values.astype(jnp.bfloat16)
    low = (values - high.astype(jnp.float32)).astype(jnp.bfloat16)
    return high, low


def swap_kernel(pieces, mine_ref, other_ref, send_sem, recv_sem):
    partner = 1 - lax.axis_index("bas")
    barrier = pltpu.get_barrier_semaphore()
    pl.semaphore_signal(barrier, inc=1, device_id={"bas": partner}, device_id_type=MESH)
    pl.semaphore_wait(barrier, 1)
    rows = mine_ref.shape[0] // pieces
    copies = []
    for piece in range(pieces):
        part = pl.ds(piece * rows, rows)
        copy = pltpu.make_async_remote_copy(
            src_ref=mine_ref.at[part],
            dst_ref=other_ref.at[part],
            send_sem=send_sem.at[piece],
            recv_sem=recv_sem.at[piece],
            device_id={"bas": partner},
            device_id_type=MESH,
        )
        copy.start()
        copies.append(copy)
    for copy in copies:
        copy.wait()


def swap(mine):
    return pl.pallas_call(
        functools.partial(swap_kernel, PIECES),
        out_shape=jax.ShapeDtypeStruct(mine.shape, mine.dtype),
        in_specs=[pl.BlockSpec(memory_space=pl.ANY)],
        out_specs=pl.BlockSpec(memory_space=pl.ANY),
        scratch_shapes=[
            pltpu.SemaphoreType.DMA((PIECES,)),
            pltpu.SemaphoreType.DMA((PIECES,)),
        ],
        compiler_params=pltpu.CompilerParams(collective_id=0, has_side_effects=True),
        name="swap_coeff",
    )(mine)


def half_kernel(
    lists_ref, counts_ref, core_ref, tile_ref, mine_ref, other_ref, half_ref, rows_ref, sem
):
    task = pl.program_id(0)
    tasks = pl.num_programs(0)
    listed = lists_ref.shape[1]
    width = tile_ref.shape[0]
    local_blocks = mine_ref.shape[0] // width

    def fetch(which):
        slot = lax.rem(which, 2)
        for index in range(listed):
            block = lists_ref[which, index]
            owner = (block >= local_blocks).astype(jnp.int32)
            first = pl.multiple_of((block - owner * local_blocks) * width, width)
            place = rows_ref.at[slot, pl.ds(index * width, width)]

            @pl.when(owner == core_ref[0])
            def _():
                pltpu.make_async_copy(
                    mine_ref.at[pl.ds(first, width)], place, sem.at[slot]
                ).start()

            @pl.when(owner != core_ref[0])
            def _():
                pltpu.make_async_copy(
                    other_ref.at[pl.ds(first, width)], place, sem.at[slot]
                ).start()

    @pl.when(task == 0)
    def _():
        fetch(task)

    @pl.when(task + 1 < tasks)
    def _():
        fetch(task + 1)

    slot = lax.rem(task, 2)
    pltpu.make_async_copy(rows_ref.at[slot], rows_ref.at[slot], sem.at[slot]).wait()
    column = lax.broadcasted_iota(jnp.int32, tile_ref.shape, 1)
    tile = jnp.where(column < counts_ref[task] * width, tile_ref[...], 0.0)
    tile_high, tile_low = split(tile)
    row_high, row_low = split(rows_ref[slot])
    both = jnp.dot(
        jnp.concatenate([tile_high, tile_low], axis=0),
        row_high,
        preferred_element_type=jnp.float32,
    )
    cross = jnp.dot(tile_high, row_low, preferred_element_type=jnp.float32)
    half_ref[...] = both[:width] + (both[width:] + cross)


def half_all(tiles, counts, lists, mine, other):
    aux_local, shell_local, width, span = tiles.shape
    tasks = aux_local * shell_local
    occupied = mine.shape[1]
    core = lax.axis_index("bas").astype(jnp.int32).reshape(1)
    return pl.pallas_call(
        half_kernel,
        out_shape=jax.ShapeDtypeStruct((shell_local * width, aux_local * occupied), jnp.float32),
        grid_spec=pltpu.PrefetchScalarGridSpec(
            num_scalar_prefetch=3,
            grid=(tasks,),
            in_specs=[
                pl.BlockSpec((width, span), lambda task, *_: (task, 0)),
                pl.BlockSpec(memory_space=pl.ANY),
                pl.BlockSpec(memory_space=pl.ANY),
            ],
            out_specs=pl.BlockSpec(
                (width, occupied), lambda task, *_: (task % shell_local, task // shell_local)
            ),
            scratch_shapes=[
                pltpu.VMEM((2, span, occupied), jnp.float32),
                pltpu.SemaphoreType.DMA((2,)),
            ],
        ),
        compiler_params=pltpu.CompilerParams(vmem_limit_bytes=VMEM_LIMIT),
        name="half_transform",
    )(
        lists.reshape(tasks, lists.shape[2]),
        counts.reshape(tasks),
        core,
        tiles.reshape(tasks * width, span),
        mine,
        other,
    )


def exchange_kernel(
    aux,
    mine_ref,
    out_ref,
    other_ref,
    parts_ref,
    near_send,
    near_recv,
    sums_ref,
    far_recv,
    turn_send,
    turn_recv,
    half_sems,
    near_sems,
    far_sems,
    turn_sems,
):
    near_count = 2
    far_count = aux // near_count
    ring = aux // 2
    keep = ring // 2
    block = out_ref.shape[0]
    half_rows = mine_ref.shape[0]

    position = lax.axis_index("aux")
    core = lax.axis_index("bas")
    far = position // near_count
    near = lax.rem(position, near_count)

    barrier = pltpu.get_barrier_semaphore()
    me = position * 2 + core
    for step in range(1, 2 * aux):
        there = lax.rem(me + step, 2 * aux)
        pl.semaphore_signal(
            barrier,
            inc=1,
            device_id={"aux": there // 2, "bas": lax.rem(there, 2)},
            device_id_type=MESH,
        )
    pl.semaphore_wait(barrier, 2 * aux - 1)

    def remote(source, target, sems, index, device):
        return pltpu.make_async_remote_copy(
            src_ref=source,
            dst_ref=target,
            send_sem=sems.at[(0,) + index],
            recv_sem=sems.at[(1,) + index],
            device_id=device,
            device_id_type=MESH,
        )

    def half_copy(index):
        part = pl.ds(index * block, block)
        return remote(
            mine_ref.at[part], other_ref.at[part], half_sems, (index,), {"bas": 1 - core}
        )

    def near_copy(step, k):
        return remote(
            near_send.at[step, k],
            near_recv.at[step, k],
            near_sems,
            (step, k),
            {"aux": far * near_count + (1 - near)},
        )

    def far_copy(target, k):
        down = (target < far).astype(jnp.int32)
        last = down * (target == far - 1).astype(jnp.int32)
        place = target + last * (far_count - target)
        return pltpu.make_async_remote_copy(
            src_ref=sums_ref.at[target, k],
            dst_ref=far_recv.at[place, k],
            send_sem=far_sems.at[0, target, k],
            recv_sem=far_sems.at[1, place, k],
            device_id={"aux": (far + 1 - 2 * down) * near_count + near},
            device_id_type=MESH,
        )

    def add_far(place, k, target):
        pltpu.make_async_copy(
            far_recv.at[place, k], far_recv.at[place, k], far_sems.at[1, place, k]
        ).wait()
        sums_ref[target, k] += far_recv[place, k]

    def target_at(step):
        upper = (far >= far_count // 2).astype(jnp.int32)
        low = far + upper * (far_count - 1 - 2 * far)
        beyond = far_count - 1 - low
        first = (step < beyond).astype(jnp.int32)
        own = (step == far_count - 1).astype(jnp.int32)
        target = (
            first * (far_count - 1 - step)
            + (1 - first) * (1 - own) * (step - beyond)
            + own * low
        )
        return target + upper * (far_count - 1 - 2 * target)

    def in_half(far_index):
        return far_index // (far_count // 2) == core

    def column_of(row, k):
        local = lax.rem(row, ring)
        inside = (row // ring == core).astype(jnp.int32)
        return lax.rem(
            inside * (local + k) + (1 - inside) * (local - k - core + 2 * ring), ring
        )

    def turn_copy(k):
        inside = in_half(far).astype(jnp.int32)
        return remote(
            turn_send.at[k],
            turn_recv.at[k],
            turn_sems,
            (k,),
            {
                "aux": core * ring + column_of(position, k),
                "bas": inside * core + (1 - inside) * (1 - core),
            },
        )

    def blocks(far_index, work):
        for k in range(keep):
            work(k)
        pl.when(in_half(far_index))(functools.partial(work, keep))

    def store_parts(source, first, index):
        part = pl.ds(pl.multiple_of(index * block, block), block)
        high, low = split(source[part, :])
        start = pl.multiple_of((first + index) * 2 * block, 2 * block)
        parts_ref[pl.ds(start, block), :] = high
        parts_ref[pl.ds(start + block, block), :] = low

    def product(row, k):
        column = core * ring + column_of(row, k)
        row_at = pl.multiple_of(row * 2 * block, 2 * block)
        column_at = pl.multiple_of(column * 2 * block, 2 * block)
        contract = (((1,), (1,)), ((), ()))
        both = lax.dot_general(
            parts_ref[pl.ds(row_at, 2 * block), :],
            parts_ref[pl.ds(column_at, block), :],
            contract,
            preferred_element_type=jnp.float32,
        )
        cross = lax.dot_general(
            parts_ref[pl.ds(row_at, block), :],
            parts_ref[pl.ds(column_at + block, block), :],
            contract,
            preferred_element_type=jnp.float32,
        )
        return both[:block] + (both[block:] + cross)

    half_blocks = half_rows // block
    for index in range(half_blocks):
        half_copy(index).start()

    def split_mine(index, carry):
        store_parts(mine_ref, core * ring, index)
        return carry

    lax.fori_loop(0, half_blocks, split_mine, 0)

    def split_other(index, carry):
        half_copy(index).wait_recv()
        store_parts(other_ref, (1 - core) * ring, index)
        return carry

    lax.fori_loop(0, half_blocks, split_other, 0)

    def send_near(step, carry):
        target = target_at(step)
        row = target * near_count + (1 - near)

        def work(k):
            near_send[target, k] = product(row, k)
            near_copy(target, k).start()

        blocks(target, work)
        return carry

    lax.fori_loop(0, far_count, send_near, 0)

    def own_products(step, carry):
        target = target_at(step)

        def work(k):
            sums_ref[target, k] = product(target * near_count + near, k)

        blocks(target, work)
        return carry

    lax.fori_loop(0, far_count, own_products, 0)

    def send_far(step, carry):
        target = target_at(step)
        between = jnp.logical_or(
            jnp.logical_and(target > far, far > 0),
            jnp.logical_and(target < far, far < far_count - 1),
        )

        def work(k):
            near_copy(target, k).wait_recv()
            sums_ref[target, k] += near_recv[target, k]

            @pl.when(between)
            def _():
                add_far(target, k, target)

            far_copy(target, k).start()

        blocks(target, work)
        return carry

    lax.fori_loop(0, far_count - 1, send_far, 0)

    def finish(k):
        near_copy(far, k).wait_recv()
        sums_ref[far, k] += near_recv[far, k]

        @pl.when(far > 0)
        def _():
            add_far(far, k, far)

        @pl.when(far < far_count - 1)
        def _():
            add_far(far_count, k, far)

        total = sums_ref[far, k]
        at = pl.multiple_of(column_of(position, k) * block, block)
        out_ref[:, pl.ds(at, block)] = total
        return total

    def turned(k):
        turn_send[k] = finish(k).T
        turn_copy(k).start()

    def place(k):
        turn_copy(k).wait_recv()
        local = lax.rem(position, ring)
        inside = in_half(far).astype(jnp.int32)
        column = lax.rem(
            inside * (local - k + ring) + (1 - inside) * (local + k + 1 - core), ring
        )
        out_ref[:, pl.ds(pl.multiple_of(column * block, block), block)] = turn_recv[k]
        turn_copy(k).wait_send()

    here = in_half(far)
    there = jnp.logical_not(here)
    for k in range(1, keep):
        turned(k)

    @pl.when(here)
    def _():
        finish(0)
        finish(keep)

    pl.when(there)(functools.partial(turned, 0))
    for k in range(1, keep):
        place(k)
    pl.when(there)(functools.partial(place, 0))

    for index in range(half_blocks):
        half_copy(index).wait_send()

    def near_done(step, carry):
        target = target_at(step)
        blocks(target, lambda k: near_copy(target, k).wait_send())
        return carry

    lax.fori_loop(0, far_count, near_done, 0)

    def far_done(step, carry):
        target = target_at(step)
        blocks(target, lambda k: far_copy(target, k).wait_send())
        return carry

    lax.fori_loop(0, far_count - 1, far_done, 0)


def exchange(half, aux):
    half_rows, depth = half.shape
    block = 2 * half_rows // aux
    far_count = aux // 2
    slots = aux // 4 + 1
    square = (block, block)
    return pl.pallas_call(
        functools.partial(exchange_kernel, aux),
        out_shape=jax.ShapeDtypeStruct((block, half_rows), jnp.float32),
        in_specs=[pl.BlockSpec(memory_space=pltpu.VMEM)],
        out_specs=pl.BlockSpec(memory_space=pltpu.VMEM),
        scratch_shapes=[
            pltpu.VMEM((half_rows, depth), jnp.float32),
            pltpu.VMEM((4 * half_rows, depth), jnp.bfloat16),
            pltpu.VMEM((far_count, slots) + square, jnp.float32),
            pltpu.VMEM((far_count, slots) + square, jnp.float32),
            pltpu.VMEM((far_count, slots) + square, jnp.float32),
            pltpu.VMEM((far_count + 1, slots) + square, jnp.float32),
            pltpu.VMEM((slots,) + square, jnp.float32),
            pltpu.VMEM((slots,) + square, jnp.float32),
            pltpu.SemaphoreType.DMA((2, half_rows // block)),
            pltpu.SemaphoreType.DMA((2, far_count, slots)),
            pltpu.SemaphoreType.DMA((2, far_count + 1, slots)),
            pltpu.SemaphoreType.DMA((2, slots)),
        ],
        compiler_params=pltpu.CompilerParams(
            collective_id=1, has_side_effects=True, vmem_limit_bytes=VMEM_LIMIT
        ),
        name="exchange",
    )(half)


def shards(aux, integrals, block_counts, partner_blocks, occupied_coeff):
    other = swap(occupied_coeff)
    half = half_all(integrals, block_counts, partner_blocks, occupied_coeff, other)
    return exchange(half, aux)


def solution(mesh):
    placed = (
        P(("grp", "aux"), "bas", None, None),
        P(("grp", "aux"), "bas"),
        P(("grp", "aux"), "bas", None),
        P(("grp", "bas"), None),
    )
    return jax.shard_map(
        functools.partial(shards, mesh.shape["aux"]),
        mesh=mesh,
        in_specs=placed,
        out_specs=P(("grp", "aux"), "bas"),
        check_vma=False,
    )
```

```python
import functools

import jax
import jax.numpy as jnp
from jax import lax
from jax.experimental import pallas as pl
from jax.experimental.pallas import tpu as pltpu
from jax.sharding import PartitionSpec as P

MESH = pl.DeviceIdType.MESH
VMEM_LIMIT = 58 * 1024 * 1024
PIECES = 10
SLOTS = 4


def split(values):
    high = values.astype(jnp.bfloat16)
    low = (values - high.astype(jnp.float32)).astype(jnp.bfloat16)
    return high, low


def exchange_kernel(
    aux,
    lists_ref,
    counts_ref,
    tiles_ref,
    coeff_ref,
    out_ref,
    land_ref,
    high_ref,
    low_ref,
    stage_ref,
    tile_ref,
    other_ref,
    parts_ref,
    near_recv,
    far_recv,
    turn_send,
    turn_recv,
    stage_sems,
    tile_sems,
    coeff_sems,
    half_sems,
    near_sems,
    far_sems,
    turn_sems,
):
    near_count = 2
    far_count = aux // near_count
    ring = aux // 2
    keep = ring // 2
    block = out_ref.shape[0]
    aux_local, shell_local, width, span = tiles_ref.shape
    tasks = aux_local * shell_local
    listed = lists_ref.shape[2]
    coeff_rows, occupied = coeff_ref.shape
    piece_rows = coeff_rows // PIECES
    slots = keep + 1
    across = occupied // block

    position = lax.axis_index("aux")
    core = lax.axis_index("bas")
    far = position // near_count
    near = lax.rem(position, near_count)

    def tile_copy(task):
        slot = lax.rem(task, SLOTS)
        return pltpu.make_async_copy(
            tiles_ref.at[task // shell_local, lax.rem(task, shell_local)],
            tile_ref.at[slot],
            tile_sems.at[slot],
        )

    def piece_at(piece):
        return pl.ds(pl.multiple_of(piece * piece_rows, piece_rows), piece_rows)

    def stage_copy(piece):
        slot = lax.rem(piece, 2)
        return pltpu.make_async_copy(
            coeff_ref.at[piece_at(piece)], stage_ref.at[slot], stage_sems.at[slot]
        )

    stage_copy(0).start()
    for task in range(SLOTS):
        tile_copy(task).start()

    barrier = pltpu.get_barrier_semaphore()
    me = position * 2 + core
    for step in range(1, 2 * aux):
        there = lax.rem(me + step, 2 * aux)
        pl.semaphore_signal(
            barrier,
            inc=1,
            device_id={"aux": there // 2, "bas": lax.rem(there, 2)},
            device_id_type=MESH,
        )
    pl.semaphore_wait(barrier, 2 * aux - 1)

    def remote(source, target, sems, index, device):
        return pltpu.make_async_remote_copy(
            src_ref=source,
            dst_ref=target,
            send_sem=sems.at[(0,) + index],
            recv_sem=sems.at[(1,) + index],
            device_id=device,
            device_id_type=MESH,
        )

    def coeff_copy(piece):
        part = piece_at(piece)
        return remote(
            coeff_ref.at[part], land_ref.at[part], coeff_sems, (piece,), {"bas": 1 - core}
        )

    def task_at(task):
        return pl.ds(pl.multiple_of(task * width, width), width)

    def half_copy(task):
        part = task_at(task)
        return remote(
            land_ref.at[part], other_ref.at[part], half_sems, (task,), {"bas": 1 - core}
        )

    def spare(number):
        row = tasks * width + (number // across) * block
        column = lax.rem(number, across) * block
        return (
            pl.ds(pl.multiple_of(row, block), block),
            pl.ds(pl.multiple_of(column, block), block),
        )

    def near_at(target, k):
        return spare(target * slots + k)

    def sum_at(target, k):
        return spare((far_count + target) * slots + k)

    def near_copy(step, k):
        return remote(
            land_ref.at[near_at(step, k)],
            near_recv.at[step, k],
            near_sems,
            (step, k),
            {"aux": far * near_count + (1 - near)},
        )

    def far_copy(target, k):
        down = (target < far).astype(jnp.int32)
        last = down * (target == far - 1).astype(jnp.int32)
        place = target + last * (far_count - target)
        return pltpu.make_async_remote_copy(
            src_ref=land_ref.at[sum_at(target, k)],
            dst_ref=far_recv.at[place, k],
            send_sem=far_sems.at[0, target, k],
            recv_sem=far_sems.at[1, place, k],
            device_id={"aux": (far + 1 - 2 * down) * near_count + near},
            device_id_type=MESH,
        )

    def add_far(place, k, target):
        pltpu.make_async_copy(
            far_recv.at[place, k], far_recv.at[place, k], far_sems.at[1, place, k]
        ).wait()
        land_ref[sum_at(target, k)] += far_recv[place, k]

    def target_at(step):
        upper = (far >= far_count // 2).astype(jnp.int32)
        low = far + upper * (far_count - 1 - 2 * far)
        beyond = far_count - 1 - low
        first = (step < beyond).astype(jnp.int32)
        own = (step == far_count - 1).astype(jnp.int32)
        target = (
            first * (far_count - 1 - step)
            + (1 - first) * (1 - own) * (step - beyond)
            + own * low
        )
        return target + upper * (far_count - 1 - 2 * target)

    def in_half(far_index):
        return far_index // (far_count // 2) == core

    def column_of(row, k):
        local = lax.rem(row, ring)
        inside = (row // ring == core).astype(jnp.int32)
        return lax.rem(
            inside * (local + k) + (1 - inside) * (local - k - core + 2 * ring), ring
        )

    def turn_copy(k):
        inside = in_half(far).astype(jnp.int32)
        return remote(
            turn_send.at[k],
            turn_recv.at[k],
            turn_sems,
            (k,),
            {
                "aux": core * ring + column_of(position, k),
                "bas": inside * core + (1 - inside) * (1 - core),
            },
        )

    def blocks(far_index, work):
        for k in range(keep):
            work(k)
        pl.when(in_half(far_index))(functools.partial(work, keep))

    def store_parts(values, half, task):
        row = half * (shell_local * width) + lax.rem(task, shell_local) * width
        start = (row // block) * 2 * block + lax.rem(row, block)
        columns = pl.ds(
            pl.multiple_of((task // shell_local) * occupied, occupied), occupied
        )
        high, low = split(values)
        parts_ref[pl.ds(pl.multiple_of(start, width), width), columns] = high
        parts_ref[pl.ds(pl.multiple_of(start + block, width), width), columns] = low

    def product(row, k):
        column = core * ring + column_of(row, k)
        row_at = pl.multiple_of(row * 2 * block, 2 * block)
        column_at = pl.multiple_of(column * 2 * block, 2 * block)
        contract = (((1,), (1,)), ((), ()))
        both = lax.dot_general(
            parts_ref[pl.ds(row_at, 2 * block), :],
            parts_ref[pl.ds(column_at, block), :],
            contract,
            preferred_element_type=jnp.float32,
        )
        cross = lax.dot_general(
            parts_ref[pl.ds(row_at, block), :],
            parts_ref[pl.ds(column_at + block, block), :],
            contract,
            preferred_element_type=jnp.float32,
        )
        return both[:block] + (both[block:] + cross)

    for piece in range(PIECES):
        coeff_copy(piece).start()

    def store_rows(values, half, piece):
        group = piece_rows // width
        first = half * (coeff_rows // width) + piece * group
        for index in range(group):
            part = values[index * width : (index + 1) * width]
            high_ref[first + index], low_ref[first + index] = split(part)

    def split_mine(piece, carry):
        pl.when(piece + 1 < PIECES)(lambda: stage_copy(piece + 1).start())
        stage_copy(piece).wait()
        store_rows(stage_ref[lax.rem(piece, 2)], core, piece)
        return carry

    lax.fori_loop(0, PIECES, split_mine, 0)

    def split_landed(piece, carry):
        coeff_copy(piece).wait_recv()
        store_rows(land_ref[piece_at(piece), :], 1 - core, piece)
        return carry

    lax.fori_loop(0, PIECES, split_landed, 0)

    def one_task(task, carry):
        tile_copy(task).wait()
        first, second = task // shell_local, lax.rem(task, shell_local)
        column = lax.broadcasted_iota(jnp.int32, (width, span), 1)
        tile = jnp.where(
            column < counts_ref[first, second] * width, tile_ref[lax.rem(task, SLOTS)], 0.0
        )
        blocks_here = [lists_ref[first, second, index] for index in range(listed)]
        row_high = jnp.concatenate([high_ref[block] for block in blocks_here], axis=0)
        row_low = jnp.concatenate([low_ref[block] for block in blocks_here], axis=0)
        tile_high, tile_low = split(tile)
        both = jnp.dot(
            jnp.concatenate([tile_high, tile_low], axis=0),
            row_high,
            preferred_element_type=jnp.float32,
        )
        cross = jnp.dot(tile_high, row_low, preferred_element_type=jnp.float32)
        half = both[:width] + (both[width:] + cross)
        land_ref[task_at(task), :] = half
        half_copy(task).start()
        store_parts(half, core, task)
        pl.when(task + SLOTS < tasks)(lambda: tile_copy(task + SLOTS).start())
        return carry

    lax.fori_loop(0, tasks, one_task, 0)

    def split_other(task, carry):
        half_copy(task).wait_recv()
        store_parts(other_ref[task_at(task), :], 1 - core, task)
        return carry

    lax.fori_loop(0, tasks, split_other, 0)

    def send_near(step, carry):
        target = target_at(step)
        row = target * near_count + (1 - near)

        def work(k):
            land_ref[near_at(target, k)] = product(row, k)
            near_copy(target, k).start()

        blocks(target, work)
        return carry

    lax.fori_loop(0, far_count, send_near, 0)

    def own_products(step, carry):
        target = target_at(step)

        def work(k):
            land_ref[sum_at(target, k)] = product(target * near_count + near, k)

        blocks(target, work)
        return carry

    lax.fori_loop(0, far_count, own_products, 0)

    def send_far(step, carry):
        target = target_at(step)
        between = jnp.logical_or(
            jnp.logical_and(target > far, far > 0),
            jnp.logical_and(target < far, far < far_count - 1),
        )

        def work(k):
            near_copy(target, k).wait_recv()
            land_ref[sum_at(target, k)] += near_recv[target, k]

            @pl.when(between)
            def _():
                add_far(target, k, target)

            far_copy(target, k).start()

        blocks(target, work)
        return carry

    lax.fori_loop(0, far_count - 1, send_far, 0)

    def finish(k):
        near_copy(far, k).wait_recv()
        land_ref[sum_at(far, k)] += near_recv[far, k]

        @pl.when(far > 0)
        def _():
            add_far(far, k, far)

        @pl.when(far < far_count - 1)
        def _():
            add_far(far_count, k, far)

        total = land_ref[sum_at(far, k)]
        at = pl.multiple_of(column_of(position, k) * block, block)
        out_ref[:, pl.ds(at, block)] = total
        return total

    def turned(k):
        turn_send[k] = finish(k).T
        turn_copy(k).start()

    def place(k):
        turn_copy(k).wait_recv()
        local = lax.rem(position, ring)
        inside = in_half(far).astype(jnp.int32)
        column = lax.rem(
            inside * (local - k + ring) + (1 - inside) * (local + k + 1 - core), ring
        )
        out_ref[:, pl.ds(pl.multiple_of(column * block, block), block)] = turn_recv[k]
        turn_copy(k).wait_send()

    here = in_half(far)
    there = jnp.logical_not(here)
    for k in range(1, keep):
        turned(k)

    @pl.when(here)
    def _():
        finish(0)
        finish(keep)

    pl.when(there)(functools.partial(turned, 0))
    for k in range(1, keep):
        place(k)
    pl.when(there)(functools.partial(place, 0))

    def coeff_done(piece, carry):
        coeff_copy(piece).wait_send()
        return carry

    lax.fori_loop(0, PIECES, coeff_done, 0)

    def half_done(task, carry):
        half_copy(task).wait_send()
        return carry

    lax.fori_loop(0, tasks, half_done, 0)

    def near_done(step, carry):
        target = target_at(step)
        blocks(target, lambda k: near_copy(target, k).wait_send())
        return carry

    lax.fori_loop(0, far_count, near_done, 0)

    def far_done(step, carry):
        target = target_at(step)
        blocks(target, lambda k: far_copy(target, k).wait_send())
        return carry

    lax.fori_loop(0, far_count - 1, far_done, 0)


def shards(aux, integrals, block_counts, partner_blocks, occupied_coeff):
    aux_local, shell_local, width, span = integrals.shape
    coeff_rows, occupied = occupied_coeff.shape
    tasks = aux_local * shell_local
    half_rows = shell_local * width
    block = 2 * half_rows // aux
    far_count = aux // 2
    slots = aux // 4 + 1
    square = (block, block)
    spares = -(-2 * far_count * slots // (occupied // block)) * block
    return pl.pallas_call(
        functools.partial(exchange_kernel, aux),
        out_shape=jax.ShapeDtypeStruct((block, half_rows), jnp.float32),
        in_specs=[
            pl.BlockSpec(memory_space=pltpu.SMEM),
            pl.BlockSpec(memory_space=pltpu.SMEM),
            pl.BlockSpec(memory_space=pl.ANY),
            pl.BlockSpec(memory_space=pl.ANY),
        ],
        out_specs=pl.BlockSpec(memory_space=pltpu.VMEM),
        scratch_shapes=[
            pltpu.VMEM((max(coeff_rows, tasks * width + spares), occupied), jnp.float32),
            pltpu.VMEM((2 * coeff_rows // width, width, occupied), jnp.bfloat16),
            pltpu.VMEM((2 * coeff_rows // width, width, occupied), jnp.bfloat16),
            pltpu.VMEM((2, coeff_rows // PIECES, occupied), jnp.float32),
            pltpu.VMEM((SLOTS, width, span), jnp.float32),
            pltpu.VMEM((tasks * width, occupied), jnp.float32),
            pltpu.VMEM((4 * half_rows, aux_local * occupied), jnp.bfloat16),
            pltpu.VMEM((far_count, slots) + square, jnp.float32),
            pltpu.VMEM((far_count + 1, slots) + square, jnp.float32),
            pltpu.VMEM((slots,) + square, jnp.float32),
            pltpu.VMEM((slots,) + square, jnp.float32),
            pltpu.SemaphoreType.DMA((2,)),
            pltpu.SemaphoreType.DMA((SLOTS,)),
            pltpu.SemaphoreType.DMA((2, PIECES)),
            pltpu.SemaphoreType.DMA((2, tasks)),
            pltpu.SemaphoreType.DMA((2, far_count, slots)),
            pltpu.SemaphoreType.DMA((2, far_count + 1, slots)),
            pltpu.SemaphoreType.DMA((2, slots)),
        ],
        compiler_params=pltpu.CompilerParams(
            collective_id=0, has_side_effects=True, vmem_limit_bytes=VMEM_LIMIT
        ),
        name="exchange",
    )(partner_blocks, block_counts, integrals, occupied_coeff)


def solution(mesh):
    placed = (
        P(("grp", "aux"), "bas", None, None),
        P(("grp", "aux"), "bas"),
        P(("grp", "aux"), "bas", None),
        P(("grp", "bas"), None),
    )
    return jax.shard_map(
        functools.partial(shards, mesh.shape["aux"]),
        mesh=mesh,
        in_specs=placed,
        out_specs=P(("grp", "aux"), "bas"),
        check_vma=False,
    )
```

```python
import functools

import jax
import jax.numpy as jnp
from jax import lax
from jax.experimental import pallas as pl
from jax.experimental.pallas import tpu as pltpu
from jax.sharding import PartitionSpec as P

MESH = pl.DeviceIdType.MESH
VMEM_LIMIT = 58 * 1024 * 1024
PIECES = 10
SLOTS = 4


def split(values):
    high = values.astype(jnp.bfloat16)
    low = (values - high.astype(jnp.float32)).astype(jnp.bfloat16)
    return high, low


def exchange_kernel(
    aux,
    lists_ref,
    counts_ref,
    tiles_ref,
    coeff_ref,
    out_ref,
    land_ref,
    high_ref,
    low_ref,
    stage_ref,
    tile_ref,
    other_ref,
    parts_ref,
    near_recv,
    far_recv,
    turn_send,
    turn_recv,
    stage_sems,
    tile_sems,
    coeff_sems,
    half_sems,
    near_sems,
    far_sems,
    turn_sems,
):
    near_count = 2
    far_count = aux // near_count
    ring = aux // 2
    keep = ring // 2
    block = out_ref.shape[0]
    aux_local, shell_local, width, span = tiles_ref.shape
    tasks = aux_local * shell_local
    listed = lists_ref.shape[2]
    coeff_rows, occupied = coeff_ref.shape
    piece_rows = coeff_rows // PIECES
    slots = keep + 1
    across = occupied // block

    position = lax.axis_index("aux")
    core = lax.axis_index("bas")
    far = position // near_count
    near = lax.rem(position, near_count)

    def tile_copy(task):
        slot = lax.rem(task, SLOTS)
        return pltpu.make_async_copy(
            tiles_ref.at[task // shell_local, lax.rem(task, shell_local)],
            tile_ref.at[slot],
            tile_sems.at[slot],
        )

    def piece_at(piece):
        return pl.ds(pl.multiple_of(piece * piece_rows, piece_rows), piece_rows)

    def stage_copy(piece):
        slot = lax.rem(piece, 2)
        return pltpu.make_async_copy(
            coeff_ref.at[piece_at(piece)], stage_ref.at[slot], stage_sems.at[slot]
        )

    stage_copy(0).start()
    for task in range(SLOTS):
        tile_copy(task).start()

    barrier = pltpu.get_barrier_semaphore()
    me = position * 2 + core
    for step in range(1, 2 * aux):
        there = lax.rem(me + step, 2 * aux)
        pl.semaphore_signal(
            barrier,
            inc=1,
            device_id={"aux": there // 2, "bas": lax.rem(there, 2)},
            device_id_type=MESH,
        )
    pl.semaphore_wait(barrier, 2 * aux - 1)

    def remote(source, target, sems, index, device):
        return pltpu.make_async_remote_copy(
            src_ref=source,
            dst_ref=target,
            send_sem=sems.at[(0,) + index],
            recv_sem=sems.at[(1,) + index],
            device_id=device,
            device_id_type=MESH,
        )

    def coeff_copy(piece):
        part = piece_at(piece)
        return remote(
            coeff_ref.at[part], land_ref.at[part], coeff_sems, (piece,), {"bas": 1 - core}
        )

    def task_at(task):
        return pl.ds(pl.multiple_of(task * width, width), width)

    def half_copy(task):
        part = task_at(task)
        return remote(
            land_ref.at[part], other_ref.at[part], half_sems, (task,), {"bas": 1 - core}
        )

    def spare(number):
        row = tasks * width + (number // across) * block
        column = lax.rem(number, across) * block
        return (
            pl.ds(pl.multiple_of(row, block), block),
            pl.ds(pl.multiple_of(column, block), block),
        )

    def near_at(target, k):
        return spare(target * slots + k)

    def sum_at(target, k):
        return spare((far_count + target) * slots + k)

    def square_at(target, k):
        return near_at(target, keep) if k == slots else sum_at(target, k)

    def near_copy(step, k):
        return remote(
            land_ref.at[near_at(step, k)],
            near_recv.at[step, k],
            near_sems,
            (step, k),
            {"aux": far * near_count + (1 - near)},
        )

    def far_copy(target, k):
        down = (target < far).astype(jnp.int32)
        last = down * (target == far - 1).astype(jnp.int32)
        place = target + last * (far_count - target)
        return pltpu.make_async_remote_copy(
            src_ref=land_ref.at[square_at(target, k)],
            dst_ref=far_recv.at[place, k],
            send_sem=far_sems.at[0, target, k],
            recv_sem=far_sems.at[1, place, k],
            device_id={"aux": (far + 1 - 2 * down) * near_count + near},
            device_id_type=MESH,
        )

    def add_far(place, k, target):
        pltpu.make_async_copy(
            far_recv.at[place, k], far_recv.at[place, k], far_sems.at[1, place, k]
        ).wait()
        land_ref[square_at(target, k)] += far_recv[place, k]

    def target_at(step):
        upper = (far >= far_count // 2).astype(jnp.int32)
        low = far + upper * (far_count - 1 - 2 * far)
        beyond = far_count - 1 - low
        first = (step < beyond).astype(jnp.int32)
        own = (step == far_count - 1).astype(jnp.int32)
        target = (
            first * (far_count - 1 - step)
            + (1 - first) * (1 - own) * (step - beyond)
            + own * low
        )
        return target + upper * (far_count - 1 - 2 * target)

    def in_half(far_index):
        return far_index // (far_count // 2) == core

    def column_of(row, k):
        local = lax.rem(row, ring)
        inside = (row // ring == core).astype(jnp.int32)
        return lax.rem(
            inside * (local + k) + (1 - inside) * (local - k - core + 2 * ring), ring
        )

    def turn_copy(k):
        inside = in_half(far).astype(jnp.int32)
        return remote(
            turn_send.at[k],
            turn_recv.at[k],
            turn_sems,
            (k,),
            {
                "aux": core * ring + column_of(position, k),
                "bas": inside * core + (1 - inside) * (1 - core),
            },
        )

    def between(target):
        return jnp.logical_or(
            jnp.logical_and(target > far, far > 0),
            jnp.logical_and(target < far, far < far_count - 1),
        )

    def gather_far(k):
        @pl.when(far > 0)
        def _():
            add_far(far, k, far)

        @pl.when(far < far_count - 1)
        def _():
            add_far(far_count, k, far)

    def store_parts(values, half, task):
        row = half * (shell_local * width) + lax.rem(task, shell_local) * width
        start = (row // block) * 2 * block + lax.rem(row, block)
        columns = pl.ds(
            pl.multiple_of((task // shell_local) * occupied, occupied), occupied
        )
        high, low = split(values)
        parts_ref[pl.ds(pl.multiple_of(start, width), width), columns] = high
        parts_ref[pl.ds(pl.multiple_of(start + block, width), width), columns] = low

    def product(row, k):
        column = core * ring + column_of(row, k)
        row_at = pl.multiple_of(row * 2 * block, 2 * block)
        column_at = pl.multiple_of(column * 2 * block, 2 * block)
        contract = (((1,), (1,)), ((), ()))
        both = lax.dot_general(
            parts_ref[pl.ds(row_at, 2 * block), :],
            parts_ref[pl.ds(column_at, block), :],
            contract,
            preferred_element_type=jnp.float32,
        )
        cross = lax.dot_general(
            parts_ref[pl.ds(row_at, block), :],
            parts_ref[pl.ds(column_at + block, block), :],
            contract,
            preferred_element_type=jnp.float32,
        )
        return both[:block] + (both[block:] + cross)

    for piece in range(PIECES):
        coeff_copy(piece).start()

    def store_rows(values, half, piece):
        group = piece_rows // width
        first = half * (coeff_rows // width) + piece * group
        for index in range(group):
            part = values[index * width : (index + 1) * width]
            high_ref[first + index], low_ref[first + index] = split(part)

    def split_mine(piece, carry):
        pl.when(piece + 1 < PIECES)(lambda: stage_copy(piece + 1).start())
        stage_copy(piece).wait()
        store_rows(stage_ref[lax.rem(piece, 2)], core, piece)
        return carry

    lax.fori_loop(0, PIECES, split_mine, 0)

    def split_landed(piece, carry):
        coeff_copy(piece).wait_recv()
        store_rows(land_ref[piece_at(piece), :], 1 - core, piece)
        return carry

    lax.fori_loop(0, PIECES, split_landed, 0)

    def one_task(task, carry):
        tile_copy(task).wait()
        first, second = task // shell_local, lax.rem(task, shell_local)
        column = lax.broadcasted_iota(jnp.int32, (width, span), 1)
        tile = jnp.where(
            column < counts_ref[first, second] * width, tile_ref[lax.rem(task, SLOTS)], 0.0
        )
        blocks_here = [lists_ref[first, second, index] for index in range(listed)]
        row_high = jnp.concatenate([high_ref[block] for block in blocks_here], axis=0)
        row_low = jnp.concatenate([low_ref[block] for block in blocks_here], axis=0)
        tile_high, tile_low = split(tile)
        both = jnp.dot(
            jnp.concatenate([tile_high, tile_low], axis=0),
            row_high,
            preferred_element_type=jnp.float32,
        )
        cross = jnp.dot(tile_high, row_low, preferred_element_type=jnp.float32)
        half = both[:width] + (both[width:] + cross)
        land_ref[task_at(task), :] = half
        half_copy(task).start()
        store_parts(half, core, task)
        pl.when(task + SLOTS < tasks)(lambda: tile_copy(task + SLOTS).start())
        return carry

    lax.fori_loop(0, tasks, one_task, 0)

    def split_other(task, carry):
        half_copy(task).wait_recv()
        store_parts(other_ref[task_at(task), :], 1 - core, task)
        return carry

    lax.fori_loop(0, tasks, split_other, 0)

    def send_near(step, carry):
        target = target_at(step)
        for k in range(keep):
            land_ref[near_at(target, k)] = product(target * near_count + (1 - near), k)
            near_copy(target, k).start()
        return carry

    lax.fori_loop(0, 1, send_near, 0)

    def start_last(step, carry):
        target = target_at(step)

        @pl.when(in_half(target))
        def _():
            for k in (keep, slots):
                index = near if k == keep else 1 - near
                land_ref[square_at(target, k)] = product(target * near_count + index, keep)

                @pl.when(jnp.logical_and(target != far, jnp.logical_not(between(target))))
                def _():
                    far_copy(target, k).start()

        return carry

    lax.fori_loop(0, far_count, start_last, 0)
    lax.fori_loop(1, far_count, send_near, 0)

    def own_products(step, carry):
        target = target_at(step)
        for k in range(keep):
            land_ref[sum_at(target, k)] = product(target * near_count + near, k)
        return carry

    lax.fori_loop(0, far_count, own_products, 0)

    def forward_last(step, carry):
        target = target_at(step)

        @pl.when(jnp.logical_and(in_half(target), between(target)))
        def _():
            for k in (keep, slots):
                add_far(target, k, target)
                far_copy(target, k).start()

        return carry

    lax.fori_loop(0, far_count - 1, forward_last, 0)

    def send_far(step, carry):
        target = target_at(step)
        for k in range(keep):
            near_copy(target, k).wait_recv()
            land_ref[sum_at(target, k)] += near_recv[target, k]

            @pl.when(between(target))
            def _():
                add_far(target, k, target)

            far_copy(target, k).start()
        return carry

    lax.fori_loop(0, 1, send_far, 0)

    @pl.when(in_half(far))
    def _():
        for k in (slots, keep):
            gather_far(k)
            if k == slots:
                near_copy(far, keep).start()

    lax.fori_loop(1, far_count - 1, send_far, 0)

    def finish(k):
        near_copy(far, k).wait_recv()
        land_ref[sum_at(far, k)] += near_recv[far, k]
        if k < keep:
            gather_far(k)
        total = land_ref[sum_at(far, k)]
        at = pl.multiple_of(column_of(position, k) * block, block)
        out_ref[:, pl.ds(at, block)] = total
        return total

    def turned(k):
        turn_send[k] = finish(k).T
        turn_copy(k).start()

    def place(k):
        turn_copy(k).wait_recv()
        local = lax.rem(position, ring)
        inside = in_half(far).astype(jnp.int32)
        column = lax.rem(
            inside * (local - k + ring) + (1 - inside) * (local + k + 1 - core), ring
        )
        out_ref[:, pl.ds(pl.multiple_of(column * block, block), block)] = turn_recv[k]
        turn_copy(k).wait_send()

    here = in_half(far)
    there = jnp.logical_not(here)
    for k in range(1, keep):
        turned(k)

    @pl.when(here)
    def _():
        finish(0)
        finish(keep)

    pl.when(there)(functools.partial(turned, 0))
    for k in range(1, keep):
        place(k)
    pl.when(there)(functools.partial(place, 0))

    def coeff_done(piece, carry):
        coeff_copy(piece).wait_send()
        return carry

    lax.fori_loop(0, PIECES, coeff_done, 0)

    def half_done(task, carry):
        half_copy(task).wait_send()
        return carry

    lax.fori_loop(0, tasks, half_done, 0)

    def near_done(step, carry):
        for k in range(keep):
            near_copy(target_at(step), k).wait_send()
        return carry

    lax.fori_loop(0, far_count, near_done, 0)
    pl.when(here)(lambda: near_copy(far, keep).wait_send())

    def far_done(step, carry):
        target = target_at(step)
        for k in range(keep):
            far_copy(target, k).wait_send()

        @pl.when(in_half(target))
        def _():
            for k in (keep, slots):
                far_copy(target, k).wait_send()

        return carry

    lax.fori_loop(0, far_count - 1, far_done, 0)


def shards(aux, integrals, block_counts, partner_blocks, occupied_coeff):
    aux_local, shell_local, width, span = integrals.shape
    coeff_rows, occupied = occupied_coeff.shape
    tasks = aux_local * shell_local
    half_rows = shell_local * width
    block = 2 * half_rows // aux
    far_count = aux // 2
    slots = aux // 4 + 1
    square = (block, block)
    spares = -(-2 * far_count * slots // (occupied // block)) * block
    return pl.pallas_call(
        functools.partial(exchange_kernel, aux),
        out_shape=jax.ShapeDtypeStruct((block, half_rows), jnp.float32),
        in_specs=[
            pl.BlockSpec(memory_space=pltpu.SMEM),
            pl.BlockSpec(memory_space=pltpu.SMEM),
            pl.BlockSpec(memory_space=pl.ANY),
            pl.BlockSpec(memory_space=pl.ANY),
        ],
        out_specs=pl.BlockSpec(memory_space=pltpu.VMEM),
        scratch_shapes=[
            pltpu.VMEM((max(coeff_rows, tasks * width + spares), occupied), jnp.float32),
            pltpu.VMEM((2 * coeff_rows // width, width, occupied), jnp.bfloat16),
            pltpu.VMEM((2 * coeff_rows // width, width, occupied), jnp.bfloat16),
            pltpu.VMEM((2, coeff_rows // PIECES, occupied), jnp.float32),
            pltpu.VMEM((SLOTS, width, span), jnp.float32),
            pltpu.VMEM((tasks * width, occupied), jnp.float32),
            pltpu.VMEM((4 * half_rows, aux_local * occupied), jnp.bfloat16),
            pltpu.VMEM((far_count, slots) + square, jnp.float32),
            pltpu.VMEM((far_count + 1, slots + 1) + square, jnp.float32),
            pltpu.VMEM((slots,) + square, jnp.float32),
            pltpu.VMEM((slots,) + square, jnp.float32),
            pltpu.SemaphoreType.DMA((2,)),
            pltpu.SemaphoreType.DMA((SLOTS,)),
            pltpu.SemaphoreType.DMA((2, PIECES)),
            pltpu.SemaphoreType.DMA((2, tasks)),
            pltpu.SemaphoreType.DMA((2, far_count, slots)),
            pltpu.SemaphoreType.DMA((2, far_count + 1, slots + 1)),
            pltpu.SemaphoreType.DMA((2, slots)),
        ],
        compiler_params=pltpu.CompilerParams(
            collective_id=0, has_side_effects=True, vmem_limit_bytes=VMEM_LIMIT
        ),
        name="exchange",
    )(partner_blocks, block_counts, integrals, occupied_coeff)


def solution(mesh):
    placed = (
        P(("grp", "aux"), "bas", None, None),
        P(("grp", "aux"), "bas"),
        P(("grp", "aux"), "bas", None),
        P(("grp", "bas"), None),
    )
    return jax.shard_map(
        functools.partial(shards, mesh.shape["aux"]),
        mesh=mesh,
        in_specs=placed,
        out_specs=P(("grp", "aux"), "bas"),
        check_vma=False,
    )
```

```python
import functools

import jax
import jax.numpy as jnp
from jax import lax
from jax.experimental import pallas as pl
from jax.experimental.pallas import tpu as pltpu
from jax.sharding import PartitionSpec as P

MESH = pl.DeviceIdType.MESH
VMEM_LIMIT = 58 * 1024 * 1024
PIECES = 10
SLOTS = 4


def split(values):
    high = values.astype(jnp.bfloat16)
    low = (values - high.astype(jnp.float32)).astype(jnp.bfloat16)
    return high, low


def exchange_kernel(
    aux,
    lists_ref,
    counts_ref,
    tiles_ref,
    coeff_ref,
    out_ref,
    land_ref,
    high_ref,
    low_ref,
    stage_ref,
    tile_ref,
    other_ref,
    parts_ref,
    near_recv,
    far_recv,
    turn_send,
    turn_recv,
    stage_sems,
    tile_sems,
    coeff_sems,
    half_sems,
    near_sems,
    far_sems,
    turn_sems,
):
    near_count = 2
    far_count = aux // near_count
    ring = aux // 2
    keep = ring // 2
    block = out_ref.shape[0]
    aux_local, shell_local, width, span = tiles_ref.shape
    tasks = aux_local * shell_local
    listed = lists_ref.shape[2]
    coeff_rows, occupied = coeff_ref.shape
    piece_rows = coeff_rows // PIECES
    slots = keep + 1
    across = occupied // block

    position = lax.axis_index("aux")
    core = lax.axis_index("bas")
    far = position // near_count
    near = lax.rem(position, near_count)

    shells = block // width
    group = shells * aux_local

    def block_of(turn):
        late = (turn >= keep).astype(jnp.int32)
        return 2 * (turn - late * keep) + late * near + (1 - late) * (1 - near)

    def task_of(order):
        inner = lax.rem(order, group)
        shell = block_of(order // group) * shells + lax.rem(inner, shells)
        return (inner // shells) * shell_local + shell

    def tile_copy(order):
        slot = lax.rem(order, SLOTS)
        task = task_of(order)
        return pltpu.make_async_copy(
            tiles_ref.at[task // shell_local, lax.rem(task, shell_local)],
            tile_ref.at[slot],
            tile_sems.at[slot],
        )

    def piece_at(piece):
        return pl.ds(pl.multiple_of(piece * piece_rows, piece_rows), piece_rows)

    def stage_copy(piece):
        slot = lax.rem(piece, 2)
        return pltpu.make_async_copy(
            coeff_ref.at[piece_at(piece)], stage_ref.at[slot], stage_sems.at[slot]
        )

    stage_copy(0).start()
    for order in range(SLOTS):
        tile_copy(jnp.int32(order)).start()

    barrier = pltpu.get_barrier_semaphore()
    me = position * 2 + core
    for step in range(1, 2 * aux):
        there = lax.rem(me + step, 2 * aux)
        pl.semaphore_signal(
            barrier,
            inc=1,
            device_id={"aux": there // 2, "bas": lax.rem(there, 2)},
            device_id_type=MESH,
        )
    pl.semaphore_wait(barrier, 2 * aux - 1)

    def remote(source, target, sems, index, device):
        return pltpu.make_async_remote_copy(
            src_ref=source,
            dst_ref=target,
            send_sem=sems.at[(0,) + index],
            recv_sem=sems.at[(1,) + index],
            device_id=device,
            device_id_type=MESH,
        )

    def coeff_copy(piece):
        part = piece_at(piece)
        return remote(
            coeff_ref.at[part], land_ref.at[part], coeff_sems, (piece,), {"bas": 1 - core}
        )

    def task_at(task):
        return pl.ds(pl.multiple_of(task * width, width), width)

    def half_copy(task):
        part = task_at(task)
        return remote(
            land_ref.at[part], other_ref.at[part], half_sems, (task,), {"bas": 1 - core}
        )

    def spare(number):
        row = tasks * width + (number // across) * block
        column = lax.rem(number, across) * block
        return (
            pl.ds(pl.multiple_of(row, block), block),
            pl.ds(pl.multiple_of(column, block), block),
        )

    def near_at(target, k):
        return spare(target * slots + k)

    def sum_at(target, k):
        return spare((far_count + target) * slots + k)

    def square_at(target, k):
        return near_at(target, keep) if k == slots else sum_at(target, k)

    def near_copy(step, k):
        return remote(
            land_ref.at[near_at(step, k)],
            near_recv.at[step, k],
            near_sems,
            (step, k),
            {"aux": far * near_count + (1 - near)},
        )

    def far_copy(target, k):
        down = (target < far).astype(jnp.int32)
        last = down * (target == far - 1).astype(jnp.int32)
        place = target + last * (far_count - target)
        return pltpu.make_async_remote_copy(
            src_ref=land_ref.at[square_at(target, k)],
            dst_ref=far_recv.at[place, k],
            send_sem=far_sems.at[0, target, k],
            recv_sem=far_sems.at[1, place, k],
            device_id={"aux": (far + 1 - 2 * down) * near_count + near},
            device_id_type=MESH,
        )

    def add_far(place, k, target):
        pltpu.make_async_copy(
            far_recv.at[place, k], far_recv.at[place, k], far_sems.at[1, place, k]
        ).wait()
        land_ref[square_at(target, k)] += far_recv[place, k]

    def target_at(step):
        upper = (far >= far_count // 2).astype(jnp.int32)
        low = far + upper * (far_count - 1 - 2 * far)
        beyond = far_count - 1 - low
        first = (step < beyond).astype(jnp.int32)
        own = (step == far_count - 1).astype(jnp.int32)
        target = (
            first * (far_count - 1 - step)
            + (1 - first) * (1 - own) * (step - beyond)
            + own * low
        )
        return target + upper * (far_count - 1 - 2 * target)

    def in_half(far_index):
        return far_index // (far_count // 2) == core

    def column_of(row, k):
        local = lax.rem(row, ring)
        inside = (row // ring == core).astype(jnp.int32)
        return lax.rem(
            inside * (local + k) + (1 - inside) * (local - k - core + 2 * ring), ring
        )

    def turn_copy(k):
        inside = in_half(far).astype(jnp.int32)
        return remote(
            turn_send.at[k],
            turn_recv.at[k],
            turn_sems,
            (k,),
            {
                "aux": core * ring + column_of(position, k),
                "bas": inside * core + (1 - inside) * (1 - core),
            },
        )

    def between(target):
        return jnp.logical_or(
            jnp.logical_and(target > far, far > 0),
            jnp.logical_and(target < far, far < far_count - 1),
        )

    def gather_far(k):
        @pl.when(far > 0)
        def _():
            add_far(far, k, far)

        @pl.when(far < far_count - 1)
        def _():
            add_far(far_count, k, far)

    def store_parts(values, half, task):
        row = half * (shell_local * width) + lax.rem(task, shell_local) * width
        start = (row // block) * 2 * block + lax.rem(row, block)
        columns = pl.ds(
            pl.multiple_of((task // shell_local) * occupied, occupied), occupied
        )
        high, low = split(values)
        parts_ref[pl.ds(pl.multiple_of(start, width), width), columns] = high
        parts_ref[pl.ds(pl.multiple_of(start + block, width), width), columns] = low

    def product(row, k):
        column = core * ring + column_of(row, k)
        row_at = pl.multiple_of(row * 2 * block, 2 * block)
        column_at = pl.multiple_of(column * 2 * block, 2 * block)
        contract = (((1,), (1,)), ((), ()))
        both = lax.dot_general(
            parts_ref[pl.ds(row_at, 2 * block), :],
            parts_ref[pl.ds(column_at, block), :],
            contract,
            preferred_element_type=jnp.float32,
        )
        cross = lax.dot_general(
            parts_ref[pl.ds(row_at, block), :],
            parts_ref[pl.ds(column_at + block, block), :],
            contract,
            preferred_element_type=jnp.float32,
        )
        return both[:block] + (both[block:] + cross)

    for piece in range(PIECES):
        coeff_copy(piece).start()

    def store_rows(values, half, piece):
        group = piece_rows // width
        first = half * (coeff_rows // width) + piece * group
        for index in range(group):
            part = values[index * width : (index + 1) * width]
            high_ref[first + index], low_ref[first + index] = split(part)

    def split_mine(piece, carry):
        pl.when(piece + 1 < PIECES)(lambda: stage_copy(piece + 1).start())
        stage_copy(piece).wait()
        store_rows(stage_ref[lax.rem(piece, 2)], core, piece)
        return carry

    lax.fori_loop(0, PIECES, split_mine, 0)

    def split_landed(piece, carry):
        coeff_copy(piece).wait_recv()
        store_rows(land_ref[piece_at(piece), :], 1 - core, piece)
        return carry

    lax.fori_loop(0, PIECES, split_landed, 0)

    def one_task(order, carry):
        task = task_of(order)
        tile_copy(order).wait()
        first, second = task // shell_local, lax.rem(task, shell_local)
        column = lax.broadcasted_iota(jnp.int32, (width, span), 1)
        tile = jnp.where(
            column < counts_ref[first, second] * width, tile_ref[lax.rem(order, SLOTS)], 0.0
        )
        blocks_here = [lists_ref[first, second, index] for index in range(listed)]
        row_high = jnp.concatenate([high_ref[block] for block in blocks_here], axis=0)
        row_low = jnp.concatenate([low_ref[block] for block in blocks_here], axis=0)
        tile_high, tile_low = split(tile)
        both = jnp.dot(
            jnp.concatenate([tile_high, tile_low], axis=0),
            row_high,
            preferred_element_type=jnp.float32,
        )
        cross = jnp.dot(tile_high, row_low, preferred_element_type=jnp.float32)
        half = both[:width] + (both[width:] + cross)
        land_ref[task_at(task), :] = half
        half_copy(task).start()
        store_parts(half, core, task)
        pl.when(order + SLOTS < tasks)(lambda: tile_copy(order + SLOTS).start())
        return carry

    def one_block(turn, carry):
        lax.fori_loop(turn * group, (turn + 1) * group, one_task, 0)

        @pl.when(turn < keep)
        def _():
            row = core * ring + block_of(turn)
            target = row // near_count
            land_ref[near_at(target, 0)] = product(row, 0)
            near_copy(target, 0).start()

        return carry

    lax.fori_loop(0, ring, one_block, 0)

    def split_other(order, carry):
        task = task_of(order)
        half_copy(task).wait_recv()
        store_parts(other_ref[task_at(task), :], 1 - core, task)
        return carry

    lax.fori_loop(0, tasks, split_other, 0)

    def send_near(step, carry):
        target = target_at(step)

        def work(k):
            land_ref[near_at(target, k)] = product(target * near_count + (1 - near), k)
            near_copy(target, k).start()

        pl.when(jnp.logical_not(in_half(target)))(functools.partial(work, 0))
        for k in range(1, keep):
            work(k)
        return carry

    lax.fori_loop(0, 1, send_near, 0)

    def start_last(step, carry):
        target = target_at(step)

        @pl.when(in_half(target))
        def _():
            for k in (keep, slots):
                index = near if k == keep else 1 - near
                land_ref[square_at(target, k)] = product(target * near_count + index, keep)

                @pl.when(jnp.logical_and(target != far, jnp.logical_not(between(target))))
                def _():
                    far_copy(target, k).start()

        return carry

    lax.fori_loop(0, far_count, start_last, 0)
    lax.fori_loop(1, far_count, send_near, 0)

    def own_products(step, carry):
        target = target_at(step)
        for k in range(keep):
            land_ref[sum_at(target, k)] = product(target * near_count + near, k)
        return carry

    lax.fori_loop(0, far_count, own_products, 0)

    def forward_last(step, carry):
        target = target_at(step)

        @pl.when(jnp.logical_and(in_half(target), between(target)))
        def _():
            for k in (keep, slots):
                add_far(target, k, target)
                far_copy(target, k).start()

        return carry

    lax.fori_loop(0, far_count - 1, forward_last, 0)

    def send_far(step, carry):
        target = target_at(step)
        for k in range(keep):
            near_copy(target, k).wait_recv()
            land_ref[sum_at(target, k)] += near_recv[target, k]

            @pl.when(between(target))
            def _():
                add_far(target, k, target)

            far_copy(target, k).start()
        return carry

    lax.fori_loop(0, 1, send_far, 0)

    @pl.when(in_half(far))
    def _():
        for k in (slots, keep):
            gather_far(k)
            if k == slots:
                near_copy(far, keep).start()

    lax.fori_loop(1, far_count - 1, send_far, 0)

    def finish(k):
        near_copy(far, k).wait_recv()
        land_ref[sum_at(far, k)] += near_recv[far, k]
        if k < keep:
            gather_far(k)
        total = land_ref[sum_at(far, k)]
        at = pl.multiple_of(column_of(position, k) * block, block)
        out_ref[:, pl.ds(at, block)] = total
        return total

    def turned(k):
        turn_send[k] = finish(k).T
        turn_copy(k).start()

    def place(k):
        turn_copy(k).wait_recv()
        local = lax.rem(position, ring)
        inside = in_half(far).astype(jnp.int32)
        column = lax.rem(
            inside * (local - k + ring) + (1 - inside) * (local + k + 1 - core), ring
        )
        out_ref[:, pl.ds(pl.multiple_of(column * block, block), block)] = turn_recv[k]
        turn_copy(k).wait_send()

    here = in_half(far)
    there = jnp.logical_not(here)
    for k in range(1, keep):
        turned(k)

    @pl.when(here)
    def _():
        finish(0)
        finish(keep)

    pl.when(there)(functools.partial(turned, 0))
    for k in range(1, keep):
        place(k)
    pl.when(there)(functools.partial(place, 0))

    def coeff_done(piece, carry):
        coeff_copy(piece).wait_send()
        return carry

    lax.fori_loop(0, PIECES, coeff_done, 0)

    def half_done(task, carry):
        half_copy(task).wait_send()
        return carry

    lax.fori_loop(0, tasks, half_done, 0)

    def near_done(step, carry):
        for k in range(keep):
            near_copy(target_at(step), k).wait_send()
        return carry

    lax.fori_loop(0, far_count, near_done, 0)
    pl.when(here)(lambda: near_copy(far, keep).wait_send())

    def far_done(step, carry):
        target = target_at(step)
        for k in range(keep):
            far_copy(target, k).wait_send()

        @pl.when(in_half(target))
        def _():
            for k in (keep, slots):
                far_copy(target, k).wait_send()

        return carry

    lax.fori_loop(0, far_count - 1, far_done, 0)


def shards(aux, integrals, block_counts, partner_blocks, occupied_coeff):
    aux_local, shell_local, width, span = integrals.shape
    coeff_rows, occupied = occupied_coeff.shape
    tasks = aux_local * shell_local
    half_rows = shell_local * width
    block = 2 * half_rows // aux
    far_count = aux // 2
    slots = aux // 4 + 1
    square = (block, block)
    spares = -(-2 * far_count * slots // (occupied // block)) * block
    return pl.pallas_call(
        functools.partial(exchange_kernel, aux),
        out_shape=jax.ShapeDtypeStruct((block, half_rows), jnp.float32),
        in_specs=[
            pl.BlockSpec(memory_space=pltpu.SMEM),
            pl.BlockSpec(memory_space=pltpu.SMEM),
            pl.BlockSpec(memory_space=pl.ANY),
            pl.BlockSpec(memory_space=pl.ANY),
        ],
        out_specs=pl.BlockSpec(memory_space=pltpu.VMEM),
        scratch_shapes=[
            pltpu.VMEM((max(coeff_rows, tasks * width + spares), occupied), jnp.float32),
            pltpu.VMEM((2 * coeff_rows // width, width, occupied), jnp.bfloat16),
            pltpu.VMEM((2 * coeff_rows // width, width, occupied), jnp.bfloat16),
            pltpu.VMEM((2, coeff_rows // PIECES, occupied), jnp.float32),
            pltpu.VMEM((SLOTS, width, span), jnp.float32),
            pltpu.VMEM((tasks * width, occupied), jnp.float32),
            pltpu.VMEM((4 * half_rows, aux_local * occupied), jnp.bfloat16),
            pltpu.VMEM((far_count, slots) + square, jnp.float32),
            pltpu.VMEM((far_count + 1, slots + 1) + square, jnp.float32),
            pltpu.VMEM((slots,) + square, jnp.float32),
            pltpu.VMEM((slots,) + square, jnp.float32),
            pltpu.SemaphoreType.DMA((2,)),
            pltpu.SemaphoreType.DMA((SLOTS,)),
            pltpu.SemaphoreType.DMA((2, PIECES)),
            pltpu.SemaphoreType.DMA((2, tasks)),
            pltpu.SemaphoreType.DMA((2, far_count, slots)),
            pltpu.SemaphoreType.DMA((2, far_count + 1, slots + 1)),
            pltpu.SemaphoreType.DMA((2, slots)),
        ],
        compiler_params=pltpu.CompilerParams(
            collective_id=0, has_side_effects=True, vmem_limit_bytes=VMEM_LIMIT
        ),
        name="exchange",
    )(partner_blocks, block_counts, integrals, occupied_coeff)


def solution(mesh):
    placed = (
        P(("grp", "aux"), "bas", None, None),
        P(("grp", "aux"), "bas"),
        P(("grp", "aux"), "bas", None),
        P(("grp", "bas"), None),
    )
    return jax.shard_map(
        functools.partial(shards, mesh.shape["aux"]),
        mesh=mesh,
        in_specs=placed,
        out_specs=P(("grp", "aux"), "bas"),
        check_vma=False,
    )
```

```python
import functools

import jax
import jax.numpy as jnp
from jax import lax
from jax.experimental import pallas as pl
from jax.experimental.pallas import tpu as pltpu
from jax.sharding import PartitionSpec as P

MESH = pl.DeviceIdType.MESH
VMEM_LIMIT = 58 * 1024 * 1024
PIECES = 10
SLOTS = 4


def split(values):
    high = values.astype(jnp.bfloat16)
    low = (values - high.astype(jnp.float32)).astype(jnp.bfloat16)
    return high, low


def exchange_kernel(
    aux,
    lists_ref,
    counts_ref,
    tiles_ref,
    coeff_ref,
    out_ref,
    land_ref,
    high_ref,
    low_ref,
    stage_ref,
    tile_ref,
    other_ref,
    parts_ref,
    near_recv,
    far_recv,
    turn_send,
    turn_recv,
    stage_sems,
    tile_sems,
    coeff_sems,
    half_sems,
    near_sems,
    far_sems,
    turn_sems,
):
    near_count = 2
    far_count = aux // near_count
    ring = aux // 2
    keep = ring // 2
    block = out_ref.shape[0]
    aux_local, shell_local, width, span = tiles_ref.shape
    tasks = aux_local * shell_local
    listed = lists_ref.shape[2]
    coeff_rows, occupied = coeff_ref.shape
    piece_rows = coeff_rows // PIECES
    slots = keep + 1
    across = occupied // block

    position = lax.axis_index("aux")
    core = lax.axis_index("bas")
    far = position // near_count
    near = lax.rem(position, near_count)

    shells = block // width
    group = shells * aux_local

    def block_of(turn):
        late = (turn >= keep).astype(jnp.int32)
        return 2 * (turn - late * keep) + late * near + (1 - late) * (1 - near)

    def task_of(order):
        inner = lax.rem(order, group)
        shell = block_of(order // group) * shells + lax.rem(inner, shells)
        return (inner // shells) * shell_local + shell

    def tile_copy(order):
        slot = lax.rem(order, SLOTS)
        task = task_of(order)
        return pltpu.make_async_copy(
            tiles_ref.at[task // shell_local, lax.rem(task, shell_local)],
            tile_ref.at[slot],
            tile_sems.at[slot],
        )

    def piece_at(piece):
        return pl.ds(pl.multiple_of(piece * piece_rows, piece_rows), piece_rows)

    def stage_copy(piece):
        slot = lax.rem(piece, 2)
        return pltpu.make_async_copy(
            coeff_ref.at[piece_at(piece)], stage_ref.at[slot], stage_sems.at[slot]
        )

    stage_copy(0).start()
    for order in range(SLOTS):
        tile_copy(jnp.int32(order)).start()

    barrier = pltpu.get_barrier_semaphore()
    me = position * 2 + core
    for step in range(1, 2 * aux):
        there = lax.rem(me + step, 2 * aux)
        pl.semaphore_signal(
            barrier,
            inc=1,
            device_id={"aux": there // 2, "bas": lax.rem(there, 2)},
            device_id_type=MESH,
        )
    pl.semaphore_wait(barrier, 2 * aux - 1)

    def remote(source, target, sems, index, device):
        return pltpu.make_async_remote_copy(
            src_ref=source,
            dst_ref=target,
            send_sem=sems.at[(0,) + index],
            recv_sem=sems.at[(1,) + index],
            device_id=device,
            device_id_type=MESH,
        )

    def coeff_copy(piece):
        part = piece_at(piece)
        return remote(
            coeff_ref.at[part], land_ref.at[part], coeff_sems, (piece,), {"bas": 1 - core}
        )

    def task_at(task):
        return pl.ds(pl.multiple_of(task * width, width), width)

    def half_copy(task):
        part = task_at(task)
        return remote(
            land_ref.at[part], other_ref.at[part], half_sems, (task,), {"bas": 1 - core}
        )

    def spare(number):
        row = tasks * width + (number // across) * block
        column = lax.rem(number, across) * block
        return (
            pl.ds(pl.multiple_of(row, block), block),
            pl.ds(pl.multiple_of(column, block), block),
        )

    def near_at(target, k):
        return spare(target * slots + k)

    def sum_at(target, k):
        return spare((far_count + target) * slots + k)

    def square_at(target, k):
        return near_at(target, keep) if k == slots else sum_at(target, k)

    def near_copy(step, k):
        return remote(
            land_ref.at[near_at(step, k)],
            near_recv.at[step, k],
            near_sems,
            (step, k),
            {"aux": far * near_count + (1 - near)},
        )

    def far_copy(target, k):
        down = (target < far).astype(jnp.int32)
        last = down * (target == far - 1).astype(jnp.int32)
        place = target + last * (far_count - target)
        return pltpu.make_async_remote_copy(
            src_ref=land_ref.at[square_at(target, k)],
            dst_ref=far_recv.at[place, k],
            send_sem=far_sems.at[0, target, k],
            recv_sem=far_sems.at[1, place, k],
            device_id={"aux": (far + 1 - 2 * down) * near_count + near},
            device_id_type=MESH,
        )

    def add_far(place, k, target):
        pltpu.make_async_copy(
            far_recv.at[place, k], far_recv.at[place, k], far_sems.at[1, place, k]
        ).wait()
        land_ref[square_at(target, k)] += far_recv[place, k]

    def target_at(step):
        upper = (far >= far_count // 2).astype(jnp.int32)
        low = far + upper * (far_count - 1 - 2 * far)
        beyond = far_count - 1 - low
        first = (step < beyond).astype(jnp.int32)
        own = (step == far_count - 1).astype(jnp.int32)
        target = (
            first * (far_count - 1 - step)
            + (1 - first) * (1 - own) * (step - beyond)
            + own * low
        )
        return target + upper * (far_count - 1 - 2 * target)

    def in_half(far_index):
        return far_index // (far_count // 2) == core

    def column_of(row, k):
        local = lax.rem(row, ring)
        inside = (row // ring == core).astype(jnp.int32)
        return lax.rem(
            inside * (local + k) + (1 - inside) * (local - k - core + 2 * ring), ring
        )

    def turn_copy(k):
        inside = in_half(far).astype(jnp.int32)
        return remote(
            turn_send.at[k],
            turn_recv.at[k],
            turn_sems,
            (k,),
            {
                "aux": core * ring + column_of(position, k),
                "bas": inside * core + (1 - inside) * (1 - core),
            },
        )

    def between(target):
        return jnp.logical_or(
            jnp.logical_and(target > far, far > 0),
            jnp.logical_and(target < far, far < far_count - 1),
        )

    def gather_far(k):
        @pl.when(far > 0)
        def _():
            add_far(far, k, far)

        @pl.when(far < far_count - 1)
        def _():
            add_far(far_count, k, far)

    def store_parts(values, half, task):
        row = half * (shell_local * width) + lax.rem(task, shell_local) * width
        start = (row // block) * 2 * block + lax.rem(row, block)
        columns = pl.ds(
            pl.multiple_of((task // shell_local) * occupied, occupied), occupied
        )
        high, low = split(values)
        parts_ref[pl.ds(pl.multiple_of(start, width), width), columns] = high
        parts_ref[pl.ds(pl.multiple_of(start + block, width), width), columns] = low

    def product(row, k):
        column = core * ring + column_of(row, k)
        row_at = pl.multiple_of(row * 2 * block, 2 * block)
        column_at = pl.multiple_of(column * 2 * block, 2 * block)
        contract = (((1,), (1,)), ((), ()))
        both = lax.dot_general(
            parts_ref[pl.ds(row_at, 2 * block), :],
            parts_ref[pl.ds(column_at, block), :],
            contract,
            preferred_element_type=jnp.float32,
        )
        cross = lax.dot_general(
            parts_ref[pl.ds(row_at, block), :],
            parts_ref[pl.ds(column_at + block, block), :],
            contract,
            preferred_element_type=jnp.float32,
        )
        return both[:block] + (both[block:] + cross)

    for piece in range(PIECES):
        coeff_copy(piece).start()

    def store_rows(values, half, piece):
        group = piece_rows // width
        first = half * (coeff_rows // width) + piece * group
        for index in range(group):
            part = values[index * width : (index + 1) * width]
            high_ref[first + index], low_ref[first + index] = split(part)

    def split_mine(piece, carry):
        pl.when(piece + 1 < PIECES)(lambda: stage_copy(piece + 1).start())
        stage_copy(piece).wait()
        store_rows(stage_ref[lax.rem(piece, 2)], core, piece)
        return carry

    lax.fori_loop(0, PIECES, split_mine, 0)

    def split_landed(piece, carry):
        coeff_copy(piece).wait_recv()
        store_rows(land_ref[piece_at(piece), :], 1 - core, piece)
        return carry

    lax.fori_loop(0, PIECES, split_landed, 0)

    def one_task(order, carry):
        task = task_of(order)
        tile_copy(order).wait()
        first, second = task // shell_local, lax.rem(task, shell_local)
        column = lax.broadcasted_iota(jnp.int32, (width, span), 1)
        tile = jnp.where(
            column < counts_ref[first, second] * width, tile_ref[lax.rem(order, SLOTS)], 0.0
        )
        blocks_here = [lists_ref[first, second, index] for index in range(listed)]
        row_high = jnp.concatenate([high_ref[block] for block in blocks_here], axis=0)
        row_low = jnp.concatenate([low_ref[block] for block in blocks_here], axis=0)
        tile_high, tile_low = split(tile)
        both = jnp.dot(
            jnp.concatenate([tile_high, tile_low], axis=0),
            row_high,
            preferred_element_type=jnp.float32,
        )
        cross = jnp.dot(tile_high, row_low, preferred_element_type=jnp.float32)
        half = both[:width] + (both[width:] + cross)
        land_ref[task_at(task), :] = half
        half_copy(task).start()
        store_parts(half, core, task)
        pl.when(order + SLOTS < tasks)(lambda: tile_copy(order + SLOTS).start())
        return carry

    def start_last(k):
        index = near if k == keep else 1 - near

        def start(step, carry):
            target = target_at(step)

            @pl.when(in_half(target))
            def _():
                land_ref[square_at(target, k)] = product(target * near_count + index, keep)

                @pl.when(jnp.logical_and(target != far, jnp.logical_not(between(target))))
                def _():
                    far_copy(target, k).start()

            return carry

        lax.fori_loop(0, far_count, start, 0)

    def one_block(turn, carry):
        lax.fori_loop(turn * group, (turn + 1) * group, one_task, 0)

        @pl.when(turn < keep)
        def _():
            row = core * ring + block_of(turn)
            target = row // near_count
            land_ref[near_at(target, 0)] = product(row, 0)
            near_copy(target, 0).start()

        pl.when(turn == keep - 1)(lambda: start_last(slots))
        return carry

    lax.fori_loop(0, ring, one_block, 0)
    start_last(keep)

    def split_other(order, carry):
        task = task_of(order)
        half_copy(task).wait_recv()
        store_parts(other_ref[task_at(task), :], 1 - core, task)
        return carry

    lax.fori_loop(0, tasks, split_other, 0)

    def send_near(step, carry):
        target = target_at(step)

        def work(k):
            land_ref[near_at(target, k)] = product(target * near_count + (1 - near), k)
            near_copy(target, k).start()

        pl.when(jnp.logical_not(in_half(target)))(functools.partial(work, 0))
        for k in range(1, keep):
            work(k)
        return carry

    lax.fori_loop(0, far_count, send_near, 0)

    def forward_last(step, carry):
        target = target_at(step)

        @pl.when(jnp.logical_and(in_half(target), between(target)))
        def _():
            for k in (slots, keep):
                add_far(target, k, target)
                far_copy(target, k).start()

        return carry

    lax.fori_loop(0, far_count - 1, forward_last, 0)

    def own_products(step, carry):
        target = target_at(step)
        for k in range(keep):
            land_ref[sum_at(target, k)] = product(target * near_count + near, k)
        return carry

    lax.fori_loop(0, far_count, own_products, 0)

    def send_far(step, carry):
        target = target_at(step)
        for k in range(keep):
            near_copy(target, k).wait_recv()
            land_ref[sum_at(target, k)] += near_recv[target, k]

            @pl.when(between(target))
            def _():
                add_far(target, k, target)

            far_copy(target, k).start()
        return carry

    lax.fori_loop(0, 1, send_far, 0)

    @pl.when(in_half(far))
    def _():
        for k in (slots, keep):
            gather_far(k)
            if k == slots:
                near_copy(far, keep).start()

    lax.fori_loop(1, far_count - 1, send_far, 0)

    def finish(k):
        near_copy(far, k).wait_recv()
        land_ref[sum_at(far, k)] += near_recv[far, k]
        if k < keep:
            gather_far(k)
        total = land_ref[sum_at(far, k)]
        at = pl.multiple_of(column_of(position, k) * block, block)
        out_ref[:, pl.ds(at, block)] = total
        return total

    def turned(k):
        turn_send[k] = finish(k).T
        turn_copy(k).start()

    def place(k):
        turn_copy(k).wait_recv()
        local = lax.rem(position, ring)
        inside = in_half(far).astype(jnp.int32)
        column = lax.rem(
            inside * (local - k + ring) + (1 - inside) * (local + k + 1 - core), ring
        )
        out_ref[:, pl.ds(pl.multiple_of(column * block, block), block)] = turn_recv[k]
        turn_copy(k).wait_send()

    here = in_half(far)
    there = jnp.logical_not(here)
    for k in range(1, keep):
        turned(k)

    @pl.when(here)
    def _():
        finish(0)
        finish(keep)

    pl.when(there)(functools.partial(turned, 0))
    for k in range(1, keep):
        place(k)
    pl.when(there)(functools.partial(place, 0))

    def coeff_done(piece, carry):
        coeff_copy(piece).wait_send()
        return carry

    lax.fori_loop(0, PIECES, coeff_done, 0)

    def half_done(task, carry):
        half_copy(task).wait_send()
        return carry

    lax.fori_loop(0, tasks, half_done, 0)

    def near_done(step, carry):
        for k in range(keep):
            near_copy(target_at(step), k).wait_send()
        return carry

    lax.fori_loop(0, far_count, near_done, 0)
    pl.when(here)(lambda: near_copy(far, keep).wait_send())

    def far_done(step, carry):
        target = target_at(step)
        for k in range(keep):
            far_copy(target, k).wait_send()

        @pl.when(in_half(target))
        def _():
            for k in (keep, slots):
                far_copy(target, k).wait_send()

        return carry

    lax.fori_loop(0, far_count - 1, far_done, 0)


def shards(aux, integrals, block_counts, partner_blocks, occupied_coeff):
    aux_local, shell_local, width, span = integrals.shape
    coeff_rows, occupied = occupied_coeff.shape
    tasks = aux_local * shell_local
    half_rows = shell_local * width
    block = 2 * half_rows // aux
    far_count = aux // 2
    slots = aux // 4 + 1
    square = (block, block)
    spares = -(-2 * far_count * slots // (occupied // block)) * block
    return pl.pallas_call(
        functools.partial(exchange_kernel, aux),
        out_shape=jax.ShapeDtypeStruct((block, half_rows), jnp.float32),
        in_specs=[
            pl.BlockSpec(memory_space=pltpu.SMEM),
            pl.BlockSpec(memory_space=pltpu.SMEM),
            pl.BlockSpec(memory_space=pl.ANY),
            pl.BlockSpec(memory_space=pl.ANY),
        ],
        out_specs=pl.BlockSpec(memory_space=pltpu.VMEM),
        scratch_shapes=[
            pltpu.VMEM((max(coeff_rows, tasks * width + spares), occupied), jnp.float32),
            pltpu.VMEM((2 * coeff_rows // width, width, occupied), jnp.bfloat16),
            pltpu.VMEM((2 * coeff_rows // width, width, occupied), jnp.bfloat16),
            pltpu.VMEM((2, coeff_rows // PIECES, occupied), jnp.float32),
            pltpu.VMEM((SLOTS, width, span), jnp.float32),
            pltpu.VMEM((tasks * width, occupied), jnp.float32),
            pltpu.VMEM((4 * half_rows, aux_local * occupied), jnp.bfloat16),
            pltpu.VMEM((far_count, slots) + square, jnp.float32),
            pltpu.VMEM((far_count + 1, slots + 1) + square, jnp.float32),
            pltpu.VMEM((slots,) + square, jnp.float32),
            pltpu.VMEM((slots,) + square, jnp.float32),
            pltpu.SemaphoreType.DMA((2,)),
            pltpu.SemaphoreType.DMA((SLOTS,)),
            pltpu.SemaphoreType.DMA((2, PIECES)),
            pltpu.SemaphoreType.DMA((2, tasks)),
            pltpu.SemaphoreType.DMA((2, far_count, slots)),
            pltpu.SemaphoreType.DMA((2, far_count + 1, slots + 1)),
            pltpu.SemaphoreType.DMA((2, slots)),
        ],
        compiler_params=pltpu.CompilerParams(
            collective_id=0, has_side_effects=True, vmem_limit_bytes=VMEM_LIMIT
        ),
        name="exchange",
    )(partner_blocks, block_counts, integrals, occupied_coeff)


def solution(mesh):
    placed = (
        P(("grp", "aux"), "bas", None, None),
        P(("grp", "aux"), "bas"),
        P(("grp", "aux"), "bas", None),
        P(("grp", "bas"), None),
    )
    return jax.shard_map(
        functools.partial(shards, mesh.shape["aux"]),
        mesh=mesh,
        in_specs=placed,
        out_specs=P(("grp", "aux"), "bas"),
        check_vma=False,
    )
```
